256 devices in a mesh: slab: 64 (over z, x, core), energy: 4 (over y).
Axes of the slice: x: 4, y: 4, z: 8, core: 2. Of those that a mesh axis runs over, the one named last changes fastest.
Arguments:
- energy_sq: float32 [4], P('energy'), may hold values from 2.5 to 3.3
- broadening: float32 [4], P('energy'), may hold values from 0.05 to 0.1
- onsite: float32 [64, 192, 192], P('slab'), may hold values from -0.005051815 to 2
- coupling: float32 [64, 192, 192], P('slab'), may hold values from -0.005051815 to 0.005051815
- sigma_in: float32 [4, 64, 192, 384], P('energy', 'slab'), may hold values from -0.02 to 0.005051815
- anharmonic: float32 [64, 192, 192], P('slab'), may hold values from 0.5 to 2
- energy_pairs: int32 [4, 8, 2], P('energy'), may hold values from 0 to 3
Outputs:
- green_diag: float32 [4, 64, 192, 384], P('energy', 'slab')
- sigma_out: float32 [4, 64, 192, 384], P('energy', 'slab')
The draws below stay inside these ranges and needn't reach their ends.
All inputs are finite; a program needn't handle non-finite values.
Results may differ from the reference program's by a relative error of at most 0.0003.
Values sent between devices are 32-bit elements; how exact they have to be, the bound alone decides.
A program may use at most 128 MiB of HBM per device.

```python
import math
import jax
import jax.numpy as jnp
from jax import lax

W = 192
PAIRS = 8
SLABS = 64
ENERGIES = 4


def symmetric(values):
    return 0.5 * (values + jnp.swapaxes(values, -1, -2))


def draw_onsite(key, part):
    key_off = jax.random.fold_in(key, 11)
    key_diag = jax.random.fold_in(key, 12)
    bound_off = 0.07 / math.sqrt(W)
    off_part = symmetric(jax.random.uniform(key_off, (SLABS, W, W), jnp.float32, -bound_off, bound_off))
    diag_part = jax.random.uniform(key_diag, (SLABS, W), jnp.float32, 1.7, 2.0)
    identity = jnp.eye(W, dtype=jnp.float32)
    return off_part * (1.0 - identity) + diag_part[:, :, None] * identity


def draw_sigma_in(key, part):
    key_real = jax.random.fold_in(key, 21)
    key_imag = jax.random.fold_in(key, 22)
    key_diag = jax.random.fold_in(key, 23)
    bound_real = 0.07 / math.sqrt(W)
    real_part = symmetric(jax.random.uniform(key_real, (ENERGIES, SLABS, W, W), jnp.float32, -bound_real, bound_real))
    bound_imag = 0.02 / W
    identity = jnp.eye(W, dtype=jnp.float32)
    imag_off = symmetric(jax.random.uniform(key_imag, (ENERGIES, SLABS, W, W), jnp.float32, -bound_imag, bound_imag)) * (1.0 - identity)
    imag_diag = jax.random.uniform(key_diag, (ENERGIES, SLABS, W), jnp.float32, -0.02, 0.0)
    imag_part = imag_off + imag_diag[..., :, None] * identity
    return jnp.concatenate([real_part, imag_part], -1)


def set_ends(values, rng, smallest, high):
    longest = values.shape.index(max(values.shape))
    spots = []
    for shift in (0, 1):
        where = [jax.random.randint(jax.random.fold_in(rng, axis), (), 0, length) for axis, length in enumerate(values.shape)]
        where[longest] = (where[longest] + shift) % values.shape[longest]
        spots.append(tuple(where))
    return values.at[spots[0]].set(smallest).at[spots[1]].set(high)


def levels(rng, dims, pieces, least, top_value):
    def one(dim, shards_of):
        steps = jax.random.uniform(jax.random.fold_in(jax.random.fold_in(rng, 6), dim), (shards_of,), jnp.float32, least / len(pieces), top_value / len(pieces))
        return jnp.repeat(jnp.exp(steps), dims[dim] // shards_of).reshape((-1,) + (1,) * (len(dims) - dim - 1))

    level = one(*pieces[0])
    for cut in pieces[1:]:
        level = level * one(*cut)
    return level


def setup_inputs(seed: int = 0) -> dict:
    key_list = jax.random.split(jax.random.key(seed), 8)
    energy_sq = jnp.clip(2.5 + 0.79999995 * jax.random.uniform(key_list[0], (ENERGIES,), jnp.float32) ** levels(key_list[0], (ENERGIES,), ((0, 4),), -0.2, 0.2), 2.5, 3.3)
    broadening = jnp.clip(jnp.exp(math.log(0.1) - 0.6931472 * jax.random.uniform(key_list[1], (ENERGIES,), jnp.float32) ** levels(key_list[1], (ENERGIES,), ((0, 4),), -0.2, 0.2)), 0.05, 0.1)
    onsite = draw_onsite(jax.random.fold_in(key_list[7], 71), 0)
    coupling = jnp.clip(jax.random.uniform(key_list[3], (SLABS, W, W), jnp.float32, -0.005051815, 0.005051815) * levels(key_list[3], (SLABS, W, W), ((0, 64),), -0.4, 0.0), -0.005051815, 0.005051815)
    sigma_in = draw_sigma_in(jax.random.fold_in(key_list[7], 71), 0)
    anharmonic = jnp.clip(jnp.exp(math.log(2.0) - 1.3862944 * jax.random.uniform(key_list[5], (SLABS, W, W), jnp.float32) ** levels(key_list[5], (SLABS, W, W), ((0, 64),), -0.2, 0.2)), 0.5, 2.0)
    energy_pairs = set_ends(jax.random.randint(key_list[6], (ENERGIES, PAIRS, 2), 0, ENERGIES), jax.random.fold_in(key_list[6], 1), 0, ENERGIES - 1).astype(jnp.int32)
    return {"energy_sq": energy_sq, "broadening": broadening, "onsite": onsite, "coupling": coupling, "sigma_in": sigma_in, "anharmonic": anharmonic, "energy_pairs": energy_pairs}


def complex_product(left, right):
    block_width = left.shape[-2]
    left_real = left[..., :block_width]
    left_imag = left[..., block_width:]
    right_real = right[..., :block_width]
    right_imag = right[..., block_width:]
    high = lax.Precision.HIGHEST
    real_part = jnp.einsum('...ij,...jk->...ik', left_real, right_real, precision=high) - jnp.einsum('...ij,...jk->...ik', left_imag, right_imag, precision=high)
    imag_part = jnp.einsum('...ij,...jk->...ik', left_real, right_imag, precision=high) + jnp.einsum('...ij,...jk->...ik', left_imag, right_real, precision=high)
    return jnp.concatenate([real_part, imag_part], -1)

def invert(matrix):
    block_width = matrix.shape[-2]
    high = lax.Precision.HIGHEST
    real_part = matrix[..., :block_width]
    imag_part = matrix[..., block_width:]
    real_part = 0.5 * (real_part + jnp.swapaxes(real_part, -1, -2))
    imag_part = 0.5 * (imag_part + jnp.swapaxes(imag_part, -1, -2))
    identity = jnp.broadcast_to(jnp.eye(block_width, dtype=jnp.float32), real_part.shape)
    imag_factor = jnp.linalg.cholesky(imag_part)
    factor_inverse = jax.scipy.linalg.solve_triangular(imag_factor, identity, lower=True)
    factor_trans = jnp.swapaxes(factor_inverse, -1, -2)
    middle = jnp.einsum('...ij,...jk,...kl->...il', factor_inverse, real_part, factor_trans, precision=high)
    middle = 0.5 * (middle + jnp.swapaxes(middle, -1, -2))
    squared = jnp.einsum('...ij,...jk->...ik', middle, middle, precision=high) + identity
    square_factor = jnp.linalg.cholesky(squared)
    right_side = jax.scipy.linalg.cho_solve((square_factor, True), factor_inverse)
    first_real = jnp.einsum('...ij,...jk,...kl->...il', factor_trans, middle, right_side, precision=high)
    first_imag = -jnp.einsum('...ij,...jk->...ik', factor_trans, right_side, precision=high)
    first = jnp.concatenate([first_real, first_imag], -1)
    first = 2.0 * first - complex_product(first, complex_product(matrix, first))
    return first

def from_below(stack, distance):
    return jnp.concatenate([jnp.zeros_like(stack[:distance]), stack[:-distance]], 0)

def from_above(stack, distance):
    return jnp.concatenate([stack[distance:], jnp.zeros_like(stack[:distance])], 0)

def reference(energy_sq, broadening, onsite, coupling, sigma_in, anharmonic, energy_pairs):
    slab_count = onsite.shape[0]
    block_width = onsite.shape[-1]
    identity = jnp.eye(block_width, dtype=jnp.float32)
    blank = jnp.zeros((slab_count, block_width, block_width), jnp.float32)
    bond_block = identity[None] + coupling
    bond_below = jnp.concatenate([jnp.zeros_like(bond_block[:1]), bond_block[:-1]], 0)
    upper_start = jnp.concatenate([-bond_block, blank], -1)
    lower_start = jnp.concatenate([-jnp.swapaxes(bond_below, 1, 2), blank], -1)

    def solve_energy(inputs):
        squared, damping, self_part = inputs
        diag_real = squared * identity[None] - onsite - self_part[..., :block_width]
        diag_imag = damping * identity[None] - self_part[..., block_width:]
        matrix = jnp.concatenate([diag_real, diag_imag], -1)
        lower_block = lower_start
        upper_block = upper_start
        distance = 1
        while distance < slab_count:
            inverse = invert(matrix)
            forward = complex_product(inverse, upper_block)
            backward = complex_product(inverse, lower_block)
            matrix = matrix - complex_product(lower_block, from_below(forward, distance)) - complex_product(upper_block, from_above(backward, distance))
            if 2 * distance < slab_count:
                new_lower = -complex_product(lower_block, from_below(backward, distance))
                new_upper = -complex_product(upper_block, from_above(forward, distance))
                lower_block = new_lower
                upper_block = new_upper
            distance = distance * 2
        return invert(matrix)
    green_diag = lax.map(solve_energy, (energy_sq, broadening, sigma_in))
    pair_count = energy_pairs.shape[1]
    scale = anharmonic / pair_count

    def target_sigma(index_table):

        def add_pair(carry, index_row):
            first = green_diag[index_row[0]]
            second = green_diag[index_row[1]]
            real_part = first[..., :block_width] * second[..., :block_width] - first[..., block_width:] * second[..., block_width:]
            imag_part = first[..., :block_width] * second[..., block_width:] + first[..., block_width:] * second[..., :block_width]
            return (carry + jnp.concatenate([real_part, imag_part], -1), None)
        summed, unused = lax.scan(add_pair, jnp.zeros((slab_count, block_width, 2 * block_width), jnp.float32), index_table)
        return jnp.concatenate([summed[..., :block_width] * scale, summed[..., block_width:] * scale], -1)
    sigma_out = lax.map(target_sigma, energy_pairs)
    return (green_diag, sigma_out)
```

```python
import functools

import jax
import jax.numpy as jnp
from jax import lax
from jax.experimental import pallas as pl
from jax.experimental.pallas import tpu as pltpu
from jax.sharding import PartitionSpec as P

MESH = pl.DeviceIdType.MESH
HALF = 64
TILES = 3
WIDTH = HALF * TILES


def dot(left, right):
    return lax.dot_general(
        left,
        right,
        (((1,), (0,)), ((), ())),
        precision=lax.Precision.HIGH,
        preferred_element_type=jnp.float32,
    )


def lanes_of(rows):
    return lax.broadcasted_iota(jnp.int32, (rows, 128), 1)


def times_i(tile):
    swapped = pltpu.roll(tile, 64, 1)
    return jnp.where(lanes_of(tile.shape[0]) < 64, -swapped, swapped)


def stacked(rows):
    return jnp.concatenate([rows, times_i(rows)], 0)


def row(tile, index):
    return jnp.broadcast_to(tile[index : index + 1, :], tile.shape)


def lane(tile, index):
    return jnp.broadcast_to(tile[:, index : index + 1], tile.shape)


def invert_eight(real, imag, sub):
    real, imag = list(real), list(imag)
    for j in range(8):
        pivot_real, pivot_imag = row(real[j], j), row(imag[j], j)
        scale = 1.0 / (pivot_real * pivot_real + pivot_imag * pivot_imag)
        inv_real, inv_imag = pivot_real * scale, -(pivot_imag * scale)
        own = sub == j
        col_real = real[j] - jnp.where(own, 1.0, 0.0)
        col_imag = imag[j]
        for k in range(8):
            if k == j:
                continue
            row_real, row_imag = row(real[k], j), row(imag[k], j)
            q_real = row_real * inv_real - row_imag * inv_imag
            q_imag = row_real * inv_imag + row_imag * inv_real
            real[k], imag[k] = (
                real[k] - col_real * q_real + col_imag * q_imag,
                imag[k] - col_real * q_imag - col_imag * q_real,
            )
        z_real = jnp.where(own, 1.0, -real[j])
        z_imag = jnp.where(own, 0.0, -imag[j])
        real[j], imag[j] = (
            z_real * inv_real - z_imag * inv_imag,
            z_real * inv_imag + z_imag * inv_real,
        )
    return real, imag


def sweep(panel):
    lanes = lanes_of(8)
    sub = lax.broadcasted_iota(jnp.int32, (8, 128), 0)
    for o in range(0, HALF, 8):
        pivot = panel[o : o + 8]
        real, imag = invert_eight(
            [lane(pivot, o + c) for c in range(8)], [lane(pivot, 64 + o + c) for c in range(8)], sub
        )
        unit = jnp.where(lanes == o + sub, 1.0, 0.0)
        unit_i = jnp.where(lanes == 64 + o + sub, 1.0, 0.0)
        inside = ((lanes >= o) & (lanes < o + 8)) | ((lanes >= 64 + o) & (lanes < 72 + o))
        rows = jnp.where(inside, unit, pivot)
        rows_i = times_i(rows)
        scaled = scaled_i = None
        for c in range(8):
            x, y = row(rows, c), row(rows_i, c)
            a, b = real[c] * x + imag[c] * y, real[c] * y - imag[c] * x
            scaled = a if c == 0 else scaled + a
            scaled_i = b if c == 0 else scaled_i + b
        parts = [jnp.zeros((o, 128), jnp.float32)] if o else []
        parts += [-(scaled + unit), jnp.zeros((56, 128), jnp.float32), -(scaled_i + unit_i)]
        parts += [jnp.zeros((56 - o, 128), jnp.float32)] if o < 56 else []
        after = panel + dot(panel, jnp.concatenate(parts, 0))
        panel = jnp.concatenate(([after[:o]] if o else []) + [scaled, after[o + 8 :]], 0)
    return panel


def invert(block):
    def step(k, carry):
        k1 = lax.rem(k + 1, 3)
        k2 = lax.rem(k + 2, 3)
        own = [pl.ds(pl.multiple_of(t * HALF, HALF), HALF) for t in (k, k1, k2)]
        panel = sweep(jnp.concatenate([block[k, r, :] for r in own], 0))
        rows = jnp.concatenate([stacked(block[k1, own[0], :]), stacked(block[k2, own[0], :])], 1)
        change = dot(panel, rows)
        for i, r in enumerate(own):
            block[k, r, :] = panel[HALF * i : HALF * (i + 1)]
            for j, t in enumerate((k1, k2)):
                part = change[HALF * i : HALF * (i + 1), 128 * j : 128 * (j + 1)]
                block[t, r, :] = part if i == 0 else block[t, r, :] + part
        return carry

    lax.fori_loop(0, 3, step, 0)


def left_of(ref):
    return jnp.concatenate([ref[t] for t in range(TILES)], 1)


def right_tile(tile):
    return jnp.concatenate([stacked(tile[HALF * t : HALF * (t + 1)]) for t in range(TILES)], 0)


def pack(real, imag):
    out = []
    for t in range(TILES):
        out.append(jnp.concatenate([real[:, HALF * t : HALF * (t + 1)], imag[:, HALF * t : HALF * (t + 1)]], 1))
    return out


def store_wide(out, tiles):
    low = lanes_of(WIDTH) < 64
    t0, t1, t2 = tiles
    out[:, 0:128] = jnp.where(low, t0, pltpu.roll(t1, 64, 1))
    out[:, 128:256] = jnp.where(low, t2, t0)
    out[:, 256:384] = jnp.where(low, pltpu.roll(t1, 64, 1), t2)


def load_wide(ref):
    low = lanes_of(WIDTH) < 64
    a, b, c = ref[:, 0:128], ref[:, 128:256], ref[:, 256:384]
    return [
        jnp.where(low, a, b),
        jnp.where(low, pltpu.roll(a, 64, 1), pltpu.roll(c, 64, 1)),
        jnp.where(low, b, c),
    ]


def kernel(
    slabs,
    energies,
    energy_ref,
    broad_ref,
    onsite_ref,
    coupling_ref,
    sigma_ref,
    anharmonic_ref,
    pairs_ref,
    green_ref,
    out_ref,
    below_ref,
    a_ref,
    x_ref,
    lower_ref,
    upper_ref,
    p_ref,
    q_ref,
    p_low,
    q_low,
    p_high,
    q_high,
    all_ref,
    bond_sems,
    send_sems,
    recv_sems,
    gather_sems,
):
    me = lax.axis_index("slab")
    point = lax.axis_index("energy")
    levels = slabs.bit_length() - 1
    barrier = pltpu.get_barrier_semaphore()
    for level in range(levels):
        h = 2**level
        for there, ok in ((me + h, me + h < slabs), (me - h, me >= h)):

            @pl.when(ok)
            def _():
                pl.semaphore_signal(barrier, inc=1, device_id=(there, point), device_id_type=MESH)

    others = [lax.rem(point + d, energies) for d in range(1, energies)]
    for there in others:
        pl.semaphore_signal(barrier, inc=1, device_id=(me, there), device_id_type=MESH)
    peers = energies - 1
    for level in range(levels):
        h = 2**level
        peers = peers + jnp.where(me + h < slabs, 1, 0) + jnp.where(me >= h, 1, 0)
    pl.semaphore_wait(barrier, peers)

    def bond():
        return pltpu.make_async_remote_copy(
            src_ref=coupling_ref,
            dst_ref=below_ref,
            send_sem=bond_sems.at[0],
            recv_sem=bond_sems.at[1],
            device_id=(me + 1, point),
            device_id_type=MESH,
        )

    @pl.when(me + 1 < slabs)
    def _():
        bond().start()

    eye_tiles = []
    for t in range(TILES):
        r = lax.broadcasted_iota(jnp.int32, (WIDTH, HALF), 0)
        c = lax.broadcasted_iota(jnp.int32, (WIDTH, HALF), 1)
        eye_tiles.append(jnp.where(r == c + HALF * t, 1.0, 0.0))
    blank = jnp.zeros((WIDTH, HALF), jnp.float32)
    onsite = onsite_ref[...]
    coupling = coupling_ref[...]
    self_tiles = load_wide(sigma_ref)
    energy = energy_ref[0]
    broad = broad_ref[0]
    for t in range(TILES):
        span = slice(HALF * t, HALF * (t + 1))
        eye = eye_tiles[t]
        a_ref[t] = (
            jnp.concatenate([energy * eye - onsite[:, span], broad * eye], 1) - self_tiles[t]
        )
        upper_ref[t] = jnp.concatenate([-(eye + coupling[:, span]), blank], 1)

    def send(which, kind, tile, level, h):
        src = (p_ref, q_ref, q_ref, p_ref)[kind].at[level, tile]
        dst = (p_low, q_high, q_low, p_high)[kind].at[level, tile]
        there = me + h if kind in (0, 2) else me - h
        return pltpu.make_async_remote_copy(
            src_ref=src,
            dst_ref=dst,
            send_sem=send_sems.at[level, kind, tile],
            recv_sem=recv_sems.at[level, kind, tile],
            device_id=(there, point),
            device_id_type=MESH,
        )

    def times(left, ref, level, sign):
        for t in range(TILES):
            yield t, dot(left, right_tile(ref[level, t]))

    def body(level, h):
        for t in range(TILES):
            x_ref[t] = a_ref[t]
        invert(x_ref)
        before = level - 1
        half = h // 2

        @pl.when(level == 0)
        def _():
            @pl.when(me + 1 < slabs)
            def _():
                bond().wait_send()

            @pl.when(me >= 1)
            def _():
                bond().wait_recv()
                below = below_ref[...].T
                for t in range(TILES):
                    lower_ref[t] = jnp.concatenate(
                        [-(eye_tiles[t] + below[:, HALF * t : HALF * (t + 1)]), blank], 1
                    )

            @pl.when(me < 1)
            def _():
                for t in range(TILES):
                    lower_ref[t] = jnp.zeros((WIDTH, 128), jnp.float32)

        @pl.when((level >= 1) & (level < levels))
        def _():
            @pl.when(me >= half)
            def _():
                left = left_of(lower_ref)
                for t in range(TILES):
                    send(0, 2, t, before, half).wait_recv()
                    lower_ref[t] = -dot(left, right_tile(q_low[before, t]))

            @pl.when(me + half < slabs)
            def _():
                left = left_of(upper_ref)
                for t in range(TILES):
                    send(0, 3, t, before, half).wait_recv()
                    upper_ref[t] = -dot(left, right_tile(p_high[before, t]))

            @pl.when(me + half >= slabs)
            def _():
                for t in range(TILES):
                    upper_ref[t] = jnp.zeros((WIDTH, 128), jnp.float32)

        @pl.when(level < levels)
        def _():
            left = left_of(x_ref)
            up = me + h < slabs
            down = me >= h
            for source, ref, kind, ok in ((upper_ref, p_ref, 0, up), (lower_ref, q_ref, 1, down)):
                for t in range(TILES):
                    ref[level, t] = dot(left, right_tile(source[t]))

                @pl.when(ok)
                def _():
                    for t in range(TILES):
                        send(0, kind, t, level, h).start()

            for kind, other, ref, base, ok in (
                (0, 2, p_low, lower_ref, down),
                (1, 3, q_high, upper_ref, up),
            ):

                @pl.when(ok)
                def _():
                    left = left_of(base)
                    for t in range(TILES):
                        send(0, kind, t, level, h).wait_recv()
                        a_ref[t] = a_ref[t] - dot(left, right_tile(ref[level, t]))

            for kind, other, ok in ((0, 2, up), (1, 3, down)):

                @pl.when(ok)
                def _():
                    for t in range(TILES):
                        send(0, kind, t, level, h).wait_send()

                @pl.when(ok & (level < levels - 1))
                def _():
                    for t in range(TILES):
                        send(0, other, t, level, h).start()

        return h * 2

    lax.fori_loop(0, levels + 1, body, 1)

    def share(d):
        return pltpu.make_async_remote_copy(
            src_ref=x_ref,
            dst_ref=all_ref.at[point],
            send_sem=gather_sems.at[0, d],
            recv_sem=gather_sems.at[1, d],
            device_id=(me, others[d]),
            device_id_type=MESH,
        )

    for d in range(energies - 1):
        share(d).start()
    tiles = [x_ref[t] for t in range(TILES)]
    store_wide(green_ref, tiles)
    for t in range(TILES):
        all_ref[point, t] = tiles[t]
    for d in range(energies - 1):
        share(d).wait()

    def finish(level, h):
        @pl.when(me + h < slabs)
        def _():
            for t in range(TILES):
                send(0, 2, t, level, h).wait_send()

        @pl.when(me >= h)
        def _():
            for t in range(TILES):
                send(0, 3, t, level, h).wait_send()

        return h * 2

    lax.fori_loop(0, levels - 1, finish, 1)

    pairs = pairs_ref.shape[0]
    anharmonic = anharmonic_ref[...] * (1.0 / pairs)
    low = lanes_of(WIDTH) < 64
    outs = []
    for t in range(TILES):
        total = jnp.zeros((WIDTH, 128), jnp.float32)
        for p in range(pairs):
            first = all_ref[pairs_ref[p, 0], t]
            second = all_ref[pairs_ref[p, 1], t]
            flipped = pltpu.roll(second, 64, 1)
            other = pltpu.roll(first, 64, 1)
            total = total + jnp.where(low, first, other) * second + jnp.where(low, -other, first) * flipped
        part = anharmonic[:, HALF * t : HALF * (t + 1)]
        outs.append(total * jnp.concatenate([part, part], 1))
    store_wide(out_ref, outs)


def shards(energy_sq, broadening, onsite, coupling, sigma_in, anharmonic, energy_pairs):
    slabs, energies = lax.axis_size("slab"), lax.axis_size("energy")
    levels = slabs.bit_length() - 1
    block = (TILES, WIDTH, 128)
    vmem = pl.BlockSpec(memory_space=pltpu.VMEM)
    smem = pl.BlockSpec(memory_space=pltpu.SMEM)
    wide = jax.ShapeDtypeStruct((WIDTH, 2 * WIDTH), jnp.float32)
    buffer = pltpu.VMEM(block, jnp.float32)
    stack = pltpu.VMEM((levels,) + block, jnp.float32)
    green, sigma = pl.pallas_call(
        functools.partial(kernel, slabs, energies),
        out_shape=(wide, wide),
        in_specs=[smem, smem, vmem, vmem, vmem, vmem, smem],
        out_specs=(vmem, vmem),
        scratch_shapes=[pltpu.VMEM((WIDTH, WIDTH), jnp.float32)]
        + [buffer] * 4
        + [stack] * 6
        + [pltpu.VMEM((energies,) + block, jnp.float32)]
        + [
            pltpu.SemaphoreType.DMA((2,)),
            pltpu.SemaphoreType.DMA((levels, 4, TILES)),
            pltpu.SemaphoreType.DMA((levels, 4, TILES)),
            pltpu.SemaphoreType.DMA((2, energies - 1)),
        ],
        compiler_params=pltpu.CompilerParams(
            collective_id=0, has_side_effects=True, vmem_limit_bytes=48 * 2**20
        ),
    )(energy_sq, broadening, onsite[0], coupling[0], sigma_in[0, 0], anharmonic[0], energy_pairs[0])
    return green[None, None], sigma[None, None]


def solution(mesh):
    in_specs = (
        P("energy"),
        P("energy"),
        P("slab", None, None),
        P("slab", None, None),
        P("energy", "slab", None, None),
        P("slab", None, None),
        P("energy", None, None),
    )
    out_specs = (P("energy", "slab", None, None), P("energy", "slab", None, None))
    return jax.shard_map(shards, mesh=mesh, in_specs=in_specs, out_specs=out_specs, check_vma=False)
```

```python
import functools

import jax
import jax.numpy as jnp
from jax import lax
from jax.experimental import pallas as pl
from jax.experimental.pallas import tpu as pltpu
from jax.sharding import PartitionSpec as P

MESH = pl.DeviceIdType.MESH
HALF = 64
TILES = 3
WIDTH = HALF * TILES


def dot(left, right, precision=lax.Precision.HIGH):
    return lax.dot_general(
        left,
        right,
        (((1,), (0,)), ((), ())),
        precision=precision,
        preferred_element_type=jnp.float32,
    )


def lanes_of(rows):
    return lax.broadcasted_iota(jnp.int32, (rows, 128), 1)


def times_i(tile):
    swapped = pltpu.roll(tile, 64, 1)
    return jnp.where(lanes_of(tile.shape[0]) < 64, -swapped, swapped)


def stacked(rows):
    return jnp.concatenate([rows, times_i(rows)], 0)


def row(tile, index):
    return jnp.broadcast_to(tile[index : index + 1, :], tile.shape)


def lane(tile, index):
    return jnp.broadcast_to(tile[:, index : index + 1], tile.shape)


def tree(terms):
    terms = list(terms)
    while len(terms) > 1:
        terms = [sum(terms[i + 1 : i + 2], terms[i]) for i in range(0, len(terms), 2)]
    return terms[0]


def eliminate(real, imag, rows, rows_i, sub):
    real, imag = list(real), list(imag)
    for j in range(8):
        pivot_real, pivot_imag = row(real[j], j), row(imag[j], j)
        scale = 1.0 / (pivot_real * pivot_real + pivot_imag * pivot_imag)
        col_real, col_imag = real[j] - jnp.where(sub == j, 1.0, 0.0), imag[j]
        y_real = col_real * pivot_real + col_imag * pivot_imag
        y_imag = col_imag * pivot_real - col_real * pivot_imag
        for k in range(j + 1, 8):
            row_real, row_imag = row(real[k], j), row(imag[k], j)
            real[k], imag[k] = (
                real[k] - (y_real * row_real - y_imag * row_imag) * scale,
                imag[k] - (y_real * row_imag + y_imag * row_real) * scale,
            )
        a, b = row(rows, j), row(rows_i, j)
        rows, rows_i = rows - (y_real * a + y_imag * b) * scale, rows_i - (y_real * b - y_imag * a) * scale
    return rows, rows_i


def sweep(panel):
    lanes = lanes_of(8)
    sub = lax.broadcasted_iota(jnp.int32, (8, 128), 0)
    pivot, following = panel[0:8], panel[8:16]
    for o in range(0, HALF, 8):
        inside = ((lanes >= o) & (lanes < o + 8)) | ((lanes >= 64 + o) & (lanes < 72 + o))

        def less(part, scaled, scaled_i):
            terms = [
                lane(part, o + c) * row(scaled, c) + lane(part, 64 + o + c) * row(scaled_i, c) for c in range(8)
            ]
            return jnp.where(inside, 0.0, part) - tree(terms)

        rows = jnp.where(inside, jnp.where(lanes == o + sub, 1.0, 0.0), pivot)
        scaled, scaled_i = eliminate(
            [lane(pivot, o + c) for c in range(8)],
            [lane(pivot, 64 + o + c) for c in range(8)],
            rows,
            times_i(rows),
            sub,
        )
        known = [scaled]
        if o < HALF - 8:
            pivot = less(following, scaled, scaled_i)
            known.append(pivot)
        if o < HALF - 16:
            following = less(panel[o + 16 : o + 24], scaled, scaled_i)
            known.append(following)
        parts = [jnp.zeros((o, 128), jnp.float32)] if o else []
        parts += [-scaled, jnp.zeros((56, 128), jnp.float32), -scaled_i]
        parts += [jnp.zeros((56 - o, 128), jnp.float32)] if o < 56 else []
        kept = [jnp.where(inside, 0.0, panel[r : r + 8]) for r in range(0, panel.shape[0], 8)]
        after = jnp.concatenate(kept, 0) + dot(panel, jnp.concatenate(parts, 0), lax.Precision.HIGHEST)
        end = o + 8 * len(known)
        panel = jnp.concatenate(([after[:o]] if o else []) + known + ([after[end:]] if end < WIDTH else []), 0)
    return panel


def rows_of(block):
    return pl.ds(pl.multiple_of(block * HALF, HALF), HALF)


def apply(block, panel, order, tile):
    rows = block[tile, rows_of(order[0]), :]
    change = dot(panel, stacked(rows), lax.Precision.HIGHEST)
    for i, r in enumerate(order):
        part = change[HALF * i : HALF * (i + 1)]
        block[tile, rows_of(r), :] = part if i == 0 else block[tile, rows_of(r), :] + part


def invert(block, arrive):
    def step(k, carry):
        arrive(k)
        order = [k, lax.rem(k + 1, 3), lax.rem(k + 2, 3)]

        @pl.when(k == 1)
        def _():
            apply(block, block[0], [0, 1, 2], 1)

        @pl.when(k == 2)
        def _():
            rows = [stacked(block[2, HALF * r : HALF * (r + 1), :]) for r in (0, 1)]
            both = jnp.concatenate([block[0], block[1]], 1)
            change = dot(both, jnp.concatenate(rows, 0), lax.Precision.HIGHEST)
            block[2, 0:128, :] = change[0:128]
            block[2, 128:192, :] = block[2, 128:192, :] + change[128:192]

        panel = sweep(jnp.concatenate([block[k, rows_of(r), :] for r in order], 0))
        for i, r in enumerate(order):
            block[k, rows_of(r), :] = panel[HALF * i : HALF * (i + 1)]

        @pl.when(k >= 1)
        def _():
            apply(block, panel, order, 0)

        @pl.when(k == 2)
        def _():
            apply(block, panel, order, 1)

        return carry

    lax.fori_loop(0, 3, step, 0)


def left_of(ref):
    return jnp.concatenate([ref[t] for t in range(TILES)], 1)


def right_tile(tile):
    return jnp.concatenate([stacked(tile[HALF * t : HALF * (t + 1)]) for t in range(TILES)], 0)


def pack(real, imag):
    out = []
    for t in range(TILES):
        out.append(jnp.concatenate([real[:, HALF * t : HALF * (t + 1)], imag[:, HALF * t : HALF * (t + 1)]], 1))
    return out


def store_wide(out, tiles):
    low = lanes_of(WIDTH) < 64
    t0, t1, t2 = tiles
    out[:, 0:128] = jnp.where(low, t0, pltpu.roll(t1, 64, 1))
    out[:, 128:256] = jnp.where(low, t2, t0)
    out[:, 256:384] = jnp.where(low, pltpu.roll(t1, 64, 1), t2)


def load_wide(ref):
    low = lanes_of(WIDTH) < 64
    a, b, c = ref[:, 0:128], ref[:, 128:256], ref[:, 256:384]
    return [
        jnp.where(low, a, b),
        jnp.where(low, pltpu.roll(a, 64, 1), pltpu.roll(c, 64, 1)),
        jnp.where(low, b, c),
    ]


def kernel(
    slabs,
    energies,
    energy_ref,
    broad_ref,
    onsite_ref,
    coupling_ref,
    sigma_ref,
    anharmonic_ref,
    pairs_ref,
    green_ref,
    out_ref,
    below_ref,
    a_ref,
    x_ref,
    lower_ref,
    upper_ref,
    p_ref,
    q_ref,
    p_low,
    q_low,
    p_high,
    q_high,
    all_0,
    all_1,
    all_2,
    bond_sems,
    send_sems,
    recv_sems,
    gather_sems,
):
    everyone = (all_0, all_1, all_2)
    me = lax.axis_index("slab")
    point = lax.axis_index("energy")
    levels = slabs.bit_length() - 1
    barrier = pltpu.get_barrier_semaphore()
    for level in range(levels):
        h = 2**level
        for there, ok in ((me + h, me + h < slabs), (me - h, me >= h)):

            @pl.when(ok)
            def _():
                pl.semaphore_signal(barrier, inc=1, device_id=(there, point), device_id_type=MESH)

    others = [lax.rem(point + d, energies) for d in range(1, energies)]
    for there in others:
        pl.semaphore_signal(barrier, inc=1, device_id=(me, there), device_id_type=MESH)
    peers = energies - 1
    for level in range(levels):
        h = 2**level
        peers = peers + jnp.where(me + h < slabs, 1, 0) + jnp.where(me >= h, 1, 0)
    pl.semaphore_wait(barrier, peers)

    def bond():
        return pltpu.make_async_remote_copy(
            src_ref=coupling_ref,
            dst_ref=below_ref,
            send_sem=bond_sems.at[0],
            recv_sem=bond_sems.at[1],
            device_id=(me + 1, point),
            device_id_type=MESH,
        )

    @pl.when(me + 1 < slabs)
    def _():
        bond().start()

    eye_tiles = []
    for t in range(TILES):
        r = lax.broadcasted_iota(jnp.int32, (WIDTH, HALF), 0)
        c = lax.broadcasted_iota(jnp.int32, (WIDTH, HALF), 1)
        eye_tiles.append(jnp.where(r == c + HALF * t, 1.0, 0.0))
    blank = jnp.zeros((WIDTH, HALF), jnp.float32)
    onsite = onsite_ref[...]
    coupling = coupling_ref[...]
    self_tiles = load_wide(sigma_ref)
    energy = energy_ref[0]
    broad = broad_ref[0]
    for t in range(TILES):
        span = slice(HALF * t, HALF * (t + 1))
        eye = eye_tiles[t]
        a_ref[t] = (
            jnp.concatenate([energy * eye - onsite[:, span], broad * eye], 1) - self_tiles[t]
        )
        upper_ref[t] = jnp.concatenate([-(eye + coupling[:, span]), blank], 1)

    def clear(level, h):
        for t in range(TILES):

            @pl.when(me < h)
            def _():
                p_low[level, t] = jnp.zeros((WIDTH, 128), jnp.float32)
                q_low[level, t] = jnp.zeros((WIDTH, 128), jnp.float32)

            @pl.when(me + h >= slabs)
            def _():
                p_high[level, t] = jnp.zeros((WIDTH, 128), jnp.float32)
                q_high[level, t] = jnp.zeros((WIDTH, 128), jnp.float32)

        return h * 2

    lax.fori_loop(0, levels, clear, 1)

    def send(kind, tile, level, h):
        src = (p_ref, q_ref, q_ref, p_ref)[kind].at[level, tile]
        dst = (p_low, q_high, q_low, p_high)[kind].at[level, tile]
        there = me + h if kind in (0, 2) else me - h
        return pltpu.make_async_remote_copy(
            src_ref=src,
            dst_ref=dst,
            send_sem=send_sems.at[level, kind, tile],
            recv_sem=recv_sems.at[level, kind, tile],
            device_id=(there, point),
            device_id_type=MESH,
        )

    def body(level, h):
        before = level - 1
        half = h // 2
        low_before = (level >= 1) & (me >= half)
        high_before = (level >= 1) & (me + half < slabs)

        def arrive(k):
            @pl.when(low_before)
            def _():
                send(0, k, before, half).wait_recv()

            @pl.when(high_before)
            def _():
                send(1, k, before, half).wait_recv()

            @pl.when(level >= 1)
            def _():
                left = jnp.concatenate([left_of(lower_ref), left_of(upper_ref)], 1)
                right = jnp.concatenate([right_tile(p_low[before, k]), right_tile(q_high[before, k])], 0)
                a_ref[k] = a_ref[k] - dot(left, right)

            x_ref[k] = a_ref[k]

        invert(x_ref, arrive)

        @pl.when(level == 0)
        def _():
            @pl.when(me + 1 < slabs)
            def _():
                bond().wait_send()

            @pl.when(me >= 1)
            def _():
                bond().wait_recv()
                below = below_ref[...].T
                for t in range(TILES):
                    lower_ref[t] = jnp.concatenate(
                        [-(eye_tiles[t] + below[:, HALF * t : HALF * (t + 1)]), blank], 1
                    )

            @pl.when(me < 1)
            def _():
                for t in range(TILES):
                    lower_ref[t] = jnp.zeros((WIDTH, 128), jnp.float32)

        @pl.when(low_before & (level < levels))
        def _():
            for t in range(TILES):
                send(2, t, before, half).wait_recv()

        @pl.when(high_before & (level < levels))
        def _():
            for t in range(TILES):
                send(3, t, before, half).wait_recv()

        @pl.when((level >= 1) & (level < levels))
        def _():
            left = left_of(lower_ref)
            for t in range(TILES):
                lower_ref[t] = -dot(left, right_tile(q_low[before, t]))
            left = left_of(upper_ref)
            for t in range(TILES):
                upper_ref[t] = -dot(left, right_tile(p_high[before, t]))

        @pl.when(level < levels)
        def _():
            left = left_of(x_ref)
            up = me + h < slabs
            down = me >= h
            for t in range(TILES):
                both = dot(left, jnp.concatenate([right_tile(upper_ref[t]), right_tile(lower_ref[t])], 1))
                p_ref[level, t] = both[:, :128]
                q_ref[level, t] = both[:, 128:]

                @pl.when(up)
                def _():
                    send(0, t, level, h).start()

                @pl.when(down)
                def _():
                    send(1, t, level, h).start()

            for t in range(TILES):

                @pl.when(up & (level < levels - 1))
                def _():
                    send(2, t, level, h).start()

                @pl.when(down & (level < levels - 1))
                def _():
                    send(3, t, level, h).start()

        return h * 2

    lax.fori_loop(0, levels + 1, body, 1)

    def share(d, t):
        return pltpu.make_async_remote_copy(
            src_ref=x_ref.at[t],
            dst_ref=everyone[t].at[point],
            send_sem=gather_sems.at[0, d, t],
            recv_sem=gather_sems.at[1, d, t],
            device_id=(me, others[d]),
            device_id_type=MESH,
        )

    for t in range(TILES):
        for d in range(energies - 1):
            share(d, t).start()
    tiles = [x_ref[t] for t in range(TILES)]
    store_wide(green_ref, tiles)
    for t in range(TILES):
        everyone[t][point] = tiles[t]

    def finish(level, h):
        for t in range(TILES):
            for kind, ok in ((0, me + h < slabs), (1, me >= h)):

                @pl.when(ok)
                def _():
                    send(kind, t, level, h).wait_send()

                @pl.when(ok & (level < levels - 1))
                def _():
                    send(kind + 2, t, level, h).wait_send()

        return h * 2

    lax.fori_loop(0, levels, finish, 1)

    pairs = pairs_ref.shape[0]
    anharmonic = anharmonic_ref[...] * (1.0 / pairs)
    low = lanes_of(WIDTH) < 64
    outs = []
    for t in range(TILES):
        for d in range(energies - 1):
            share(d, t).wait()
        total = jnp.zeros((WIDTH, 128), jnp.float32)
        for p in range(pairs):
            first = everyone[t][pairs_ref[p, 0]]
            second = everyone[t][pairs_ref[p, 1]]
            flipped = pltpu.roll(second, 64, 1)
            other = pltpu.roll(first, 64, 1)
            total = total + jnp.where(low, first, other) * second + jnp.where(low, -other, first) * flipped
        part = anharmonic[:, HALF * t : HALF * (t + 1)]
        outs.append(total * jnp.concatenate([part, part], 1))
    store_wide(out_ref, outs)


def shards(energy_sq, broadening, onsite, coupling, sigma_in, anharmonic, energy_pairs):
    slabs, energies = lax.axis_size("slab"), lax.axis_size("energy")
    levels = slabs.bit_length() - 1
    block = (TILES, WIDTH, 128)
    vmem = pl.BlockSpec(memory_space=pltpu.VMEM)
    smem = pl.BlockSpec(memory_space=pltpu.SMEM)
    wide = jax.ShapeDtypeStruct((WIDTH, 2 * WIDTH), jnp.float32)
    buffer = pltpu.VMEM(block, jnp.float32)
    stack = pltpu.VMEM((levels,) + block, jnp.float32)
    green, sigma = pl.pallas_call(
        functools.partial(kernel, slabs, energies),
        out_shape=(wide, wide),
        in_specs=[smem, smem, vmem, vmem, vmem, vmem, smem],
        out_specs=(vmem, vmem),
        scratch_shapes=[pltpu.VMEM((WIDTH, WIDTH), jnp.float32)]
        + [buffer] * 4
        + [stack] * 6
        + [pltpu.VMEM((energies, WIDTH, 128), jnp.float32)] * TILES
        + [
            pltpu.SemaphoreType.DMA((2,)),
            pltpu.SemaphoreType.DMA((levels, 4, TILES)),
            pltpu.SemaphoreType.DMA((levels, 4, TILES)),
            pltpu.SemaphoreType.DMA((2, energies - 1, TILES)),
        ],
        compiler_params=pltpu.CompilerParams(
            collective_id=0, has_side_effects=True, vmem_limit_bytes=48 * 2**20
        ),
    )(energy_sq, broadening, onsite[0], coupling[0], sigma_in[0, 0], anharmonic[0], energy_pairs[0])
    return green[None, None], sigma[None, None]


def solution(mesh):
    in_specs = (
        P("energy"),
        P("energy"),
        P("slab", None, None),
        P("slab", None, None),
        P("energy", "slab", None, None),
        P("slab", None, None),
        P("energy", None, None),
    )
    out_specs = (P("energy", "slab", None, None), P("energy", "slab", None, None))
    return jax.shard_map(shards, mesh=mesh, in_specs=in_specs, out_specs=out_specs, check_vma=False)
```

```python
import functools

import jax
import jax.numpy as jnp
from jax import lax
from jax.experimental import pallas as pl
from jax.experimental.pallas import tpu as pltpu
from jax.sharding import PartitionSpec as P

MESH = pl.DeviceIdType.MESH
HALF = 64
TILES = 3
WIDTH = HALF * TILES


def dot(left, right, precision=lax.Precision.HIGH):
    return lax.dot_general(
        left,
        right,
        (((1,), (0,)), ((), ())),
        precision=precision,
        preferred_element_type=jnp.float32,
    )


def split(value):
    high = value.astype(jnp.bfloat16)
    return high, (value - high.astype(jnp.float32)).astype(jnp.bfloat16)


def dot16(left, right):
    return lax.dot_general(left, right, (((1,), (0,)), ((), ())), preferred_element_type=jnp.float32)


def product(left, right):
    left_high, left_low = left
    right_high, right_low = split(right)
    width = right.shape[1]
    both = dot16(left_high, jnp.concatenate([right_high, right_low], 1))
    return both[:, :width] + (both[:, width:] + dot16(left_low, right_high))


def lanes_of(rows):
    return lax.broadcasted_iota(jnp.int32, (rows, 128), 1)


def times_i(tile):
    swapped = pltpu.roll(tile, 64, 1)
    return jnp.where(lanes_of(tile.shape[0]) < 64, -swapped, swapped)


def stacked(rows):
    return jnp.concatenate([rows, times_i(rows)], 0)


def row(tile, index):
    return jnp.broadcast_to(tile[index : index + 1, :], tile.shape)


def lane(tile, index):
    return jnp.broadcast_to(tile[:, index : index + 1], tile.shape)


def tree(terms):
    terms = list(terms)
    while len(terms) > 1:
        terms = [sum(terms[i + 1 : i + 2], terms[i]) for i in range(0, len(terms), 2)]
    return terms[0]


def eliminate(real, imag, rows, rows_i, sub):
    real, imag = list(real), list(imag)
    for j in range(8):
        pivot_real, pivot_imag = row(real[j], j), row(imag[j], j)
        scale = 1.0 / (pivot_real * pivot_real + pivot_imag * pivot_imag)
        col_real, col_imag = real[j] - jnp.where(sub == j, 1.0, 0.0), imag[j]
        y_real = col_real * pivot_real + col_imag * pivot_imag
        y_imag = col_imag * pivot_real - col_real * pivot_imag
        for k in range(j + 1, 8):
            row_real, row_imag = row(real[k], j), row(imag[k], j)
            real[k], imag[k] = (
                real[k] - (y_real * row_real - y_imag * row_imag) * scale,
                imag[k] - (y_real * row_imag + y_imag * row_real) * scale,
            )
        a, b = row(rows, j), row(rows_i, j)
        rows, rows_i = rows - (y_real * a + y_imag * b) * scale, rows_i - (y_real * b - y_imag * a) * scale
    return rows, rows_i


def sweep(panel):
    lanes = lanes_of(8)
    sub = lax.broadcasted_iota(jnp.int32, (8, 128), 0)
    pivot, following = panel[0:8], panel[8:16]
    for o in range(0, HALF, 8):
        inside = ((lanes >= o) & (lanes < o + 8)) | ((lanes >= 64 + o) & (lanes < 72 + o))

        def less(part, scaled, scaled_i):
            terms = [
                lane(part, o + c) * row(scaled, c) + lane(part, 64 + o + c) * row(scaled_i, c) for c in range(8)
            ]
            return jnp.where(inside, 0.0, part) - tree(terms)

        rows = jnp.where(inside, jnp.where(lanes == o + sub, 1.0, 0.0), pivot)
        scaled, scaled_i = eliminate(
            [lane(pivot, o + c) for c in range(8)],
            [lane(pivot, 64 + o + c) for c in range(8)],
            rows,
            times_i(rows),
            sub,
        )
        known = [scaled]
        if o < HALF - 8:
            pivot = less(following, scaled, scaled_i)
            known.append(pivot)
        if o < HALF - 16:
            following = less(panel[o + 16 : o + 24], scaled, scaled_i)
            known.append(following)
        parts = [jnp.zeros((o, 128), jnp.float32)] if o else []
        parts += [-scaled, jnp.zeros((56, 128), jnp.float32), -scaled_i]
        parts += [jnp.zeros((56 - o, 128), jnp.float32)] if o < 56 else []
        kept = [jnp.where(inside, 0.0, panel[r : r + 8]) for r in range(0, panel.shape[0], 8)]
        after = jnp.concatenate(kept, 0) + dot(panel, jnp.concatenate(parts, 0), lax.Precision.HIGHEST)
        end = o + 8 * len(known)
        panel = jnp.concatenate(([after[:o]] if o else []) + known + ([after[end:]] if end < WIDTH else []), 0)
    return panel


def rows_of(block):
    return pl.ds(pl.multiple_of(block * HALF, HALF), HALF)


def apply(block, panel, order, tile):
    rows = block[tile, rows_of(order[0]), :]
    change = product(split(panel), stacked(rows))
    for i, r in enumerate(order):
        part = change[HALF * i : HALF * (i + 1)]
        block[tile, rows_of(r), :] = part if i == 0 else block[tile, rows_of(r), :] + part


def invert(block, arrive):
    def step(k, carry):
        arrive(k)
        order = [k, lax.rem(k + 1, 3), lax.rem(k + 2, 3)]

        @pl.when(k == 1)
        def _():
            apply(block, block[0], [0, 1, 2], 1)

        @pl.when(k == 2)
        def _():
            rows = [stacked(block[2, HALF * r : HALF * (r + 1), :]) for r in (0, 1)]
            both = jnp.concatenate([block[0], block[1]], 1)
            change = product(split(both), jnp.concatenate(rows, 0))
            block[2, 0:128, :] = change[0:128]
            block[2, 128:192, :] = block[2, 128:192, :] + change[128:192]

        panel = sweep(jnp.concatenate([block[k, rows_of(r), :] for r in order], 0))
        for i, r in enumerate(order):
            block[k, rows_of(r), :] = panel[HALF * i : HALF * (i + 1)]

        @pl.when(k >= 1)
        def _():
            apply(block, panel, order, 0)

        @pl.when(k == 2)
        def _():
            apply(block, panel, order, 1)

        return carry

    lax.fori_loop(0, 3, step, 0)


def left_of(ref):
    return jnp.concatenate([ref[t] for t in range(TILES)], 1)


def right_tile(tile):
    return jnp.concatenate([stacked(tile[HALF * t : HALF * (t + 1)]) for t in range(TILES)], 0)


def pack(real, imag):
    out = []
    for t in range(TILES):
        out.append(jnp.concatenate([real[:, HALF * t : HALF * (t + 1)], imag[:, HALF * t : HALF * (t + 1)]], 1))
    return out


def store_wide(out, tiles):
    low = lanes_of(WIDTH) < 64
    t0, t1, t2 = tiles
    out[:, 0:128] = jnp.where(low, t0, pltpu.roll(t1, 64, 1))
    out[:, 128:256] = jnp.where(low, t2, t0)
    out[:, 256:384] = jnp.where(low, pltpu.roll(t1, 64, 1), t2)


def load_wide(ref):
    low = lanes_of(WIDTH) < 64
    a, b, c = ref[:, 0:128], ref[:, 128:256], ref[:, 256:384]
    return [
        jnp.where(low, a, b),
        jnp.where(low, pltpu.roll(a, 64, 1), pltpu.roll(c, 64, 1)),
        jnp.where(low, b, c),
    ]


def kernel(
    slabs,
    energies,
    energy_ref,
    broad_ref,
    onsite_ref,
    coupling_ref,
    sigma_ref,
    anharmonic_ref,
    pairs_ref,
    green_ref,
    out_ref,
    below_ref,
    a_ref,
    x_ref,
    high_ref,
    low_ref,
    x_high,
    x_low,
    p_ref,
    q_ref,
    p_low,
    q_low,
    p_high,
    q_high,
    all_0,
    all_1,
    all_2,
    bond_sems,
    send_sems,
    recv_sems,
    gather_sems,
):
    everyone = (all_0, all_1, all_2)
    me = lax.axis_index("slab")
    point = lax.axis_index("energy")
    levels = slabs.bit_length() - 1
    barrier = pltpu.get_barrier_semaphore()
    for level in range(levels):
        h = 2**level
        for there, ok in ((me + h, me + h < slabs), (me - h, me >= h)):

            @pl.when(ok)
            def _():
                pl.semaphore_signal(barrier, inc=1, device_id=(there, point), device_id_type=MESH)

    others = [lax.rem(point + d, energies) for d in range(1, energies)]
    for there in others:
        pl.semaphore_signal(barrier, inc=1, device_id=(me, there), device_id_type=MESH)
    peers = energies - 1
    for level in range(levels):
        h = 2**level
        peers = peers + jnp.where(me + h < slabs, 1, 0) + jnp.where(me >= h, 1, 0)
    pl.semaphore_wait(barrier, peers)

    @pl.when(me < 1)
    def _():
        below_ref[...] = jnp.zeros((WIDTH, WIDTH), jnp.float32)

    def bond():
        return pltpu.make_async_remote_copy(
            src_ref=coupling_ref,
            dst_ref=below_ref,
            send_sem=bond_sems.at[0],
            recv_sem=bond_sems.at[1],
            device_id=(me + 1, point),
            device_id_type=MESH,
        )

    @pl.when(me + 1 < slabs)
    def _():
        bond().start()

    eye_tiles = []
    for t in range(TILES):
        r = lax.broadcasted_iota(jnp.int32, (WIDTH, HALF), 0)
        c = lax.broadcasted_iota(jnp.int32, (WIDTH, HALF), 1)
        eye_tiles.append(jnp.where(r == c + HALF * t, 1.0, 0.0))
    blank = jnp.zeros((WIDTH, HALF), jnp.float32)
    eye_whole = jnp.concatenate(eye_tiles, 1)
    onsite = onsite_ref[...]
    self_tiles = load_wide(sigma_ref)
    energy = energy_ref[0]
    broad = broad_ref[0]
    for t in range(TILES):
        span = slice(HALF * t, HALF * (t + 1))
        eye = eye_tiles[t]
        a_ref[t] = (
            jnp.concatenate([energy * eye - onsite[:, span], broad * eye], 1) - self_tiles[t]
        )

    def clear(level, h):
        for t in range(TILES):

            @pl.when(me < h)
            def _():
                p_low[level, t] = jnp.zeros((WIDTH, 128), jnp.float32)
                q_low[level, t] = jnp.zeros((WIDTH, 128), jnp.float32)

            @pl.when(me + h >= slabs)
            def _():
                p_high[level, t] = jnp.zeros((WIDTH, 128), jnp.float32)
                q_high[level, t] = jnp.zeros((WIDTH, 128), jnp.float32)

        return h * 2

    lax.fori_loop(0, levels, clear, 1)

    def send(kind, tile, level, h):
        src = (p_ref, q_ref, q_ref, p_ref)[kind].at[level, tile]
        dst = (p_low, q_high, q_low, p_high)[kind].at[level, tile]
        there = me + h if kind in (0, 2) else me - h
        return pltpu.make_async_remote_copy(
            src_ref=src,
            dst_ref=dst,
            send_sem=send_sems.at[level, kind, tile],
            recv_sem=recv_sems.at[level, kind, tile],
            device_id=(there, point),
            device_id_type=MESH,
        )

    def body(level, h):
        before = level - 1
        half = h // 2
        low_before = (level >= 1) & (me >= half)
        high_before = (level >= 1) & (me + half < slabs)

        def arrive(k):
            @pl.when(low_before)
            def _():
                send(0, k, before, half).wait_recv()

            @pl.when(high_before)
            def _():
                send(1, k, before, half).wait_recv()

            @pl.when(level >= 1)
            def _():
                left = high_ref[lax.rem(before, 2)], low_ref[lax.rem(before, 2)]
                right = jnp.concatenate([right_tile(p_low[before, k]), right_tile(q_high[before, k])], 0)
                a_ref[k] = a_ref[k] - product(left, right)

            x_ref[k] = a_ref[k]

        invert(x_ref, arrive)
        for t in range(TILES):
            high, low = split(x_ref[t])
            x_high[:, 128 * t : 128 * (t + 1)] = high
            x_low[:, 128 * t : 128 * (t + 1)] = low

        up = me + h < slabs
        down = me >= h
        now = lax.rem(level, 2)
        then = 1 - now

        def keep(t, lower, upper):
            for base, tile in ((0, lower), (384, upper)):
                high, low = split(tile)
                high_ref[now, :, base + 128 * t : base + 128 * (t + 1)] = high
                low_ref[now, :, base + 128 * t : base + 128 * (t + 1)] = low
            both = product((x_high[...], x_low[...]), jnp.concatenate([right_tile(upper), right_tile(lower)], 1))
            p_ref[level, t] = both[:, :128]
            q_ref[level, t] = both[:, 128:]

            @pl.when(up)
            def _():
                send(0, t, level, h).start()

            @pl.when(down)
            def _():
                send(1, t, level, h).start()

        @pl.when(level == 0)
        def _():
            @pl.when(me + 1 < slabs)
            def _():
                bond().wait_send()

            @pl.when(me >= 1)
            def _():
                bond().wait_recv()

            below = jnp.where(me > 0, eye_whole + below_ref[...].T, 0.0)
            for t in range(TILES):
                span = slice(HALF * t, HALF * (t + 1))
                keep(
                    t,
                    jnp.concatenate([-below[:, span], blank], 1),
                    jnp.concatenate([-(eye_tiles[t] + coupling_ref[:, span]), blank], 1),
                )

        @pl.when((level >= 1) & (level < levels))
        def _():
            for t in range(TILES):

                @pl.when(low_before)
                def _():
                    send(2, t, before, half).wait_recv()

                @pl.when(high_before)
                def _():
                    send(3, t, before, half).wait_recv()

                keep(
                    t,
                    -product((high_ref[then, :, 0:384], low_ref[then, :, 0:384]), right_tile(q_low[before, t])),
                    -product((high_ref[then, :, 384:768], low_ref[then, :, 384:768]), right_tile(p_high[before, t])),
                )

        for t in range(TILES):

            @pl.when(up & (level < levels - 1))
            def _():
                send(2, t, level, h).start()

            @pl.when(down & (level < levels - 1))
            def _():
                send(3, t, level, h).start()

        return h * 2

    lax.fori_loop(0, levels + 1, body, 1)

    def share(d, t):
        return pltpu.make_async_remote_copy(
            src_ref=x_ref.at[t],
            dst_ref=everyone[t].at[point],
            send_sem=gather_sems.at[0, d, t],
            recv_sem=gather_sems.at[1, d, t],
            device_id=(me, others[d]),
            device_id_type=MESH,
        )

    for t in range(TILES):
        for d in range(energies - 1):
            share(d, t).start()
    tiles = [x_ref[t] for t in range(TILES)]
    store_wide(green_ref, tiles)
    for t in range(TILES):
        everyone[t][point] = tiles[t]

    def finish(level, h):
        for t in range(TILES):
            for kind, ok in ((0, me + h < slabs), (1, me >= h)):

                @pl.when(ok)
                def _():
                    send(kind, t, level, h).wait_send()

                @pl.when(ok & (level < levels - 1))
                def _():
                    send(kind + 2, t, level, h).wait_send()

        return h * 2

    lax.fori_loop(0, levels, finish, 1)

    pairs = pairs_ref.shape[0]
    anharmonic = anharmonic_ref[...] * (1.0 / pairs)
    low = lanes_of(WIDTH) < 64
    outs = []
    for t in range(TILES):
        for d in range(energies - 1):
            share(d, t).wait()
        total = jnp.zeros((WIDTH, 128), jnp.float32)
        for p in range(pairs):
            first = everyone[t][pairs_ref[p, 0]]
            second = everyone[t][pairs_ref[p, 1]]
            flipped = pltpu.roll(second, 64, 1)
            other = pltpu.roll(first, 64, 1)
            total = total + jnp.where(low, first, other) * second + jnp.where(low, -other, first) * flipped
        part = anharmonic[:, HALF * t : HALF * (t + 1)]
        outs.append(total * jnp.concatenate([part, part], 1))
    store_wide(out_ref, outs)


def shards(energy_sq, broadening, onsite, coupling, sigma_in, anharmonic, energy_pairs):
    slabs, energies = lax.axis_size("slab"), lax.axis_size("energy")
    levels = slabs.bit_length() - 1
    block = (TILES, WIDTH, 128)
    vmem = pl.BlockSpec(memory_space=pltpu.VMEM)
    smem = pl.BlockSpec(memory_space=pltpu.SMEM)
    wide = jax.ShapeDtypeStruct((WIDTH, 2 * WIDTH), jnp.float32)
    buffer = pltpu.VMEM(block, jnp.float32)
    stack = pltpu.VMEM((levels,) + block, jnp.float32)
    green, sigma = pl.pallas_call(
        functools.partial(kernel, slabs, energies),
        out_shape=(wide, wide),
        in_specs=[smem, smem, vmem, vmem, vmem, vmem, smem],
        out_specs=(vmem, vmem),
        scratch_shapes=[pltpu.VMEM((WIDTH, WIDTH), jnp.float32)]
        + [buffer] * 2
        + [pltpu.VMEM((2, WIDTH, 4 * WIDTH), jnp.bfloat16)] * 2
        + [pltpu.VMEM((WIDTH, 2 * WIDTH), jnp.bfloat16)] * 2
        + [stack] * 6
        + [pltpu.VMEM((energies, WIDTH, 128), jnp.float32)] * TILES
        + [
            pltpu.SemaphoreType.DMA((2,)),
            pltpu.SemaphoreType.DMA((levels, 4, TILES)),
            pltpu.SemaphoreType.DMA((levels, 4, TILES)),
            pltpu.SemaphoreType.DMA((2, energies - 1, TILES)),
        ],
        compiler_params=pltpu.CompilerParams(
            collective_id=0, has_side_effects=True, vmem_limit_bytes=48 * 2**20
        ),
    )(energy_sq, broadening, onsite[0], coupling[0], sigma_in[0, 0], anharmonic[0], energy_pairs[0])
    return green[None, None], sigma[None, None]


def solution(mesh):
    in_specs = (
        P("energy"),
        P("energy"),
        P("slab", None, None),
        P("slab", None, None),
        P("energy", "slab", None, None),
        P("slab", None, None),
        P("energy", None, None),
    )
    out_specs = (P("energy", "slab", None, None), P("energy", "slab", None, None))
    return jax.shard_map(shards, mesh=mesh, in_specs=in_specs, out_specs=out_specs, check_vma=False)
```

```python
import functools

import jax
import jax.numpy as jnp
from jax import lax
from jax.experimental import pallas as pl
from jax.experimental.pallas import tpu as pltpu
from jax.sharding import PartitionSpec as P

MESH = pl.DeviceIdType.MESH
HALF = 64
TILES = 3
WIDTH = HALF * TILES


def dot(left, right, precision=lax.Precision.HIGH):
    return lax.dot_general(
        left,
        right,
        (((1,), (0,)), ((), ())),
        precision=precision,
        preferred_element_type=jnp.float32,
    )


def split(value):
    high = value.astype(jnp.bfloat16)
    return high, (value - high.astype(jnp.float32)).astype(jnp.bfloat16)


def dot16(left, right):
    return lax.dot_general(left, right, (((1,), (0,)), ((), ())), preferred_element_type=jnp.float32)


def product(left, right):
    left_high, left_low = left
    right_high, right_low = split(right)
    width = right.shape[1]
    both = dot16(left_high, jnp.concatenate([right_high, right_low], 1))
    return both[:, :width] + (both[:, width:] + dot16(left_low, right_high))


def lanes_of(rows):
    return lax.broadcasted_iota(jnp.int32, (rows, 128), 1)


def times_i(tile):
    swapped = pltpu.roll(tile, 64, 1)
    return jnp.where(lanes_of(tile.shape[0]) < 64, -swapped, swapped)


def stacked(rows):
    return jnp.concatenate([rows, times_i(rows)], 0)


def row(tile, index):
    return jnp.broadcast_to(tile[index : index + 1, :], tile.shape)


def lane(tile, index):
    return jnp.broadcast_to(tile[:, index : index + 1], tile.shape)


def tree(terms):
    terms = list(terms)
    while len(terms) > 1:
        terms = [sum(terms[i + 1 : i + 2], terms[i]) for i in range(0, len(terms), 2)]
    return terms[0]


def eliminate(real, imag, rows, rows_i, sub):
    real, imag = list(real), list(imag)
    for j in range(8):
        pivot_real, pivot_imag = row(real[j], j), row(imag[j], j)
        scale = 1.0 / (pivot_real * pivot_real + pivot_imag * pivot_imag)
        col_real, col_imag = real[j] - jnp.where(sub == j, 1.0, 0.0), imag[j]
        y_real = col_real * pivot_real + col_imag * pivot_imag
        y_imag = col_imag * pivot_real - col_real * pivot_imag
        for k in range(j + 1, 8):
            row_real, row_imag = row(real[k], j), row(imag[k], j)
            real[k], imag[k] = (
                real[k] - (y_real * row_real - y_imag * row_imag) * scale,
                imag[k] - (y_real * row_imag + y_imag * row_real) * scale,
            )
        a, b = row(rows, j), row(rows_i, j)
        rows, rows_i = rows - (y_real * a + y_imag * b) * scale, rows_i - (y_real * b - y_imag * a) * scale
    return rows, rows_i


def sweep(panel):
    lanes = lanes_of(8)
    sub = lax.broadcasted_iota(jnp.int32, (8, 128), 0)
    pivot, following = panel[0:8], panel[8:16]
    for o in range(0, HALF, 8):
        inside = ((lanes >= o) & (lanes < o + 8)) | ((lanes >= 64 + o) & (lanes < 72 + o))

        def less(part, scaled, scaled_i):
            terms = [
                lane(part, o + c) * row(scaled, c) + lane(part, 64 + o + c) * row(scaled_i, c) for c in range(8)
            ]
            return jnp.where(inside, 0.0, part) - tree(terms)

        rows = jnp.where(inside, jnp.where(lanes == o + sub, 1.0, 0.0), pivot)
        scaled, scaled_i = eliminate(
            [lane(pivot, o + c) for c in range(8)],
            [lane(pivot, 64 + o + c) for c in range(8)],
            rows,
            times_i(rows),
            sub,
        )
        known = [scaled]
        if o < HALF - 8:
            pivot = less(following, scaled, scaled_i)
            known.append(pivot)
        if o < HALF - 16:
            following = less(panel[o + 16 : o + 24], scaled, scaled_i)
            known.append(following)
        parts = [jnp.zeros((o, 128), jnp.float32)] if o else []
        parts += [-scaled, jnp.zeros((56, 128), jnp.float32), -scaled_i]
        parts += [jnp.zeros((56 - o, 128), jnp.float32)] if o < 56 else []
        kept = [jnp.where(inside, 0.0, panel[r : r + 8]) for r in range(0, panel.shape[0], 8)]
        after = jnp.concatenate(kept, 0) + dot(panel, jnp.concatenate(parts, 0), lax.Precision.HIGHEST)
        end = o + 8 * len(known)
        panel = jnp.concatenate(([after[:o]] if o else []) + known + ([after[end:]] if end < WIDTH else []), 0)
    return panel


def rows_of(block):
    return pl.ds(pl.multiple_of(block * HALF, HALF), HALF)


def apply(block, panel, order, tile):
    rows = block[tile, rows_of(order[0]), :]
    change = product(split(panel), stacked(rows))
    for i, r in enumerate(order):
        part = change[HALF * i : HALF * (i + 1)]
        block[tile, rows_of(r), :] = part if i == 0 else block[tile, rows_of(r), :] + part


def invert(block, arrive):
    def step(k, carry):
        arrive(k)
        order = [k, lax.rem(k + 1, 3), lax.rem(k + 2, 3)]

        @pl.when(k == 1)
        def _():
            apply(block, block[0], [0, 1, 2], 1)

        @pl.when(k == 2)
        def _():
            rows = [stacked(block[2, HALF * r : HALF * (r + 1), :]) for r in (0, 1)]
            both = jnp.concatenate([block[0], block[1]], 1)
            change = product(split(both), jnp.concatenate(rows, 0))
            block[2, 0:128, :] = change[0:128]
            block[2, 128:192, :] = block[2, 128:192, :] + change[128:192]

        panel = sweep(jnp.concatenate([block[k, rows_of(r), :] for r in order], 0))
        for i, r in enumerate(order):
            block[k, rows_of(r), :] = panel[HALF * i : HALF * (i + 1)]

        @pl.when(k >= 1)
        def _():
            apply(block, panel, order, 0)

        @pl.when(k == 2)
        def _():
            apply(block, panel, order, 1)

        return carry

    lax.fori_loop(0, 3, step, 0)


def left_of(ref):
    return jnp.concatenate([ref[t] for t in range(TILES)], 1)


def right_tile(tile):
    return jnp.concatenate([stacked(tile[HALF * t : HALF * (t + 1)]) for t in range(TILES)], 0)


def pack(real, imag):
    out = []
    for t in range(TILES):
        out.append(jnp.concatenate([real[:, HALF * t : HALF * (t + 1)], imag[:, HALF * t : HALF * (t + 1)]], 1))
    return out


def store_wide(out, tiles):
    low = lanes_of(WIDTH) < 64
    t0, t1, t2 = tiles
    out[:, 0:128] = jnp.where(low, t0, pltpu.roll(t1, 64, 1))
    out[:, 128:256] = jnp.where(low, t2, t0)
    out[:, 256:384] = jnp.where(low, pltpu.roll(t1, 64, 1), t2)


def load_wide(ref):
    low = lanes_of(WIDTH) < 64
    a, b, c = ref[:, 0:128], ref[:, 128:256], ref[:, 256:384]
    return [
        jnp.where(low, a, b),
        jnp.where(low, pltpu.roll(a, 64, 1), pltpu.roll(c, 64, 1)),
        jnp.where(low, b, c),
    ]


def kernel(
    slabs,
    energies,
    energy_ref,
    broad_ref,
    onsite_arg,
    coupling_arg,
    sigma_arg,
    anharmonic_arg,
    pairs_ref,
    green_ref,
    out_ref,
    onsite_ref,
    coupling_ref,
    sigma_ref,
    anharmonic_ref,
    load_sems,
    below_ref,
    a_ref,
    x_ref,
    high_ref,
    low_ref,
    x_high,
    x_low,
    p_ref,
    q_ref,
    p_low,
    q_low,
    p_high,
    q_high,
    all_0,
    all_1,
    all_2,
    turned,
    bond_sems,
    send_sems,
    recv_sems,
    gather_sems,
):
    everyone = (all_0, all_1, all_2)
    me = lax.axis_index("slab")
    point = lax.axis_index("energy")
    levels = slabs.bit_length() - 1
    loads = [
        pltpu.make_async_copy(source, target, load_sems.at[i])
        for i, (source, target) in enumerate(
            (
                (coupling_arg, coupling_ref),
                (sigma_arg, sigma_ref),
                (onsite_arg, onsite_ref),
                (anharmonic_arg, anharmonic_ref),
            )
        )
    ]
    for load in loads:
        load.start()
    barrier = pltpu.get_barrier_semaphore()
    for level in range(levels):
        h = 2**level
        for there, ok in ((me + h, me + h < slabs), (me - h, me >= h)):

            @pl.when(ok)
            def _():
                pl.semaphore_signal(barrier, inc=1, device_id=(there, point), device_id_type=MESH)

    others = [lax.rem(point + d, energies) for d in range(1, energies)]
    for there in others:
        pl.semaphore_signal(barrier, inc=1, device_id=(me, there), device_id_type=MESH)
    @pl.when(me < 1)
    def _():
        below_ref[...] = jnp.zeros((WIDTH, WIDTH), jnp.float32)

    def bond():
        return pltpu.make_async_remote_copy(
            src_ref=coupling_ref,
            dst_ref=below_ref,
            send_sem=bond_sems.at[0],
            recv_sem=bond_sems.at[1],
            device_id=(me + 1, point),
            device_id_type=MESH,
        )

    eye_tiles = []
    for t in range(TILES):
        r = lax.broadcasted_iota(jnp.int32, (WIDTH, HALF), 0)
        c = lax.broadcasted_iota(jnp.int32, (WIDTH, HALF), 1)
        eye_tiles.append(jnp.where(r == c + HALF * t, 1.0, 0.0))
    blank = jnp.zeros((WIDTH, HALF), jnp.float32)
    eye_whole = jnp.concatenate(eye_tiles, 1)
    for load in loads[:3]:
        load.wait()
    onsite = onsite_ref[...]
    self_tiles = load_wide(sigma_ref)
    energy = energy_ref[0]
    broad = broad_ref[0]
    for t in range(TILES):
        span = slice(HALF * t, HALF * (t + 1))
        eye = eye_tiles[t]
        a_ref[t] = (
            jnp.concatenate([energy * eye - onsite[:, span], broad * eye], 1) - self_tiles[t]
        )

    peers = energies - 1
    for level in range(levels):
        h = 2**level
        peers = peers + jnp.where(me + h < slabs, 1, 0) + jnp.where(me >= h, 1, 0)
    pl.semaphore_wait(barrier, peers)

    @pl.when(me + 1 < slabs)
    def _():
        bond().start()

    def clear(level, h):
        for t in range(TILES):

            @pl.when(me < h)
            def _():
                p_low[level, t] = jnp.zeros((WIDTH, 128), jnp.float32)
                q_low[level, t] = jnp.zeros((WIDTH, 128), jnp.float32)

            @pl.when(me + h >= slabs)
            def _():
                p_high[level, t] = jnp.zeros((WIDTH, 128), jnp.float32)
                q_high[level, t] = jnp.zeros((WIDTH, 128), jnp.float32)

        return h * 2

    lax.fori_loop(0, levels, clear, 1)

    def send(kind, tile, level, h):
        src = (p_ref, q_ref, q_ref, p_ref)[kind].at[level, tile]
        dst = (p_low, q_high, q_low, p_high)[kind].at[level, tile]
        there = me + h if kind in (0, 2) else me - h
        return pltpu.make_async_remote_copy(
            src_ref=src,
            dst_ref=dst,
            send_sem=send_sems.at[level, kind, tile],
            recv_sem=recv_sems.at[level, kind, tile],
            device_id=(there, point),
            device_id_type=MESH,
        )

    def body(level, h):
        before = level - 1
        half = h // 2
        low_before = (level >= 1) & (me >= half)
        high_before = (level >= 1) & (me + half < slabs)

        def arrive(k):
            @pl.when(low_before)
            def _():
                send(0, k, before, half).wait_recv()

            @pl.when(high_before)
            def _():
                send(1, k, before, half).wait_recv()

            @pl.when(level >= 1)
            def _():
                left = high_ref[lax.rem(before, 2)], low_ref[lax.rem(before, 2)]
                right = jnp.concatenate([right_tile(p_low[before, k]), right_tile(q_high[before, k])], 0)
                a_ref[k] = a_ref[k] - product(left, right)

            x_ref[k] = a_ref[k]

        invert(x_ref, arrive)
        for t in range(TILES):
            high, low = split(x_ref[t])
            x_high[:, 128 * t : 128 * (t + 1)] = high
            x_low[:, 128 * t : 128 * (t + 1)] = low

        up = me + h < slabs
        down = me >= h
        now = lax.rem(level, 2)
        then = 1 - now

        def keep(t, lower, upper):
            for base, tile in ((0, lower), (384, upper)):
                high, low = split(tile)
                high_ref[now, :, base + 128 * t : base + 128 * (t + 1)] = high
                low_ref[now, :, base + 128 * t : base + 128 * (t + 1)] = low
            return jnp.concatenate([right_tile(upper), right_tile(lower)], 1)

        def spread(t, couplings):
            both = product((x_high[...], x_low[...]), couplings)
            p_ref[level, t] = both[:, :128]
            q_ref[level, t] = both[:, 128:]

        def pass_on(t):
            @pl.when(up)
            def _():
                send(0, t, level, h).start()

            @pl.when(down)
            def _():
                send(1, t, level, h).start()

        def couple(t):
            old = high_ref[then], low_ref[then]
            return keep(
                t,
                -product((old[0][:, 0:384], old[1][:, 0:384]), right_tile(q_low[before, t])),
                -product((old[0][:, 384:768], old[1][:, 384:768]), right_tile(p_high[before, t])),
            )

        @pl.when(level == 0)
        def _():
            @pl.when(me + 1 < slabs)
            def _():
                bond().wait_send()

            @pl.when(me >= 1)
            def _():
                bond().wait_recv()

            below = jnp.where(me > 0, eye_whole + below_ref[...].T, 0.0)
            for t in range(TILES):
                span = slice(HALF * t, HALF * (t + 1))
                spread(
                    t,
                    keep(
                        t,
                        jnp.concatenate([-below[:, span], blank], 1),
                        jnp.concatenate([-(eye_tiles[t] + coupling_ref[:, span]), blank], 1),
                    ),
                )
                pass_on(t)

        @pl.when((level >= 1) & (level < levels))
        def _():
            couplings = None
            for t in range(TILES):

                @pl.when(low_before)
                def _():
                    send(2, t, before, half).wait_recv()

                @pl.when(high_before)
                def _():
                    send(3, t, before, half).wait_recv()

                after = couple(t)
                if t:
                    spread(t - 1, couplings)
                    pass_on(t - 1)
                couplings = after

            spread(TILES - 1, couplings)
            pass_on(TILES - 1)

        for t in range(TILES):

            @pl.when(up & (level < levels - 1))
            def _():
                send(2, t, level, h).start()

            @pl.when(down & (level < levels - 1))
            def _():
                send(3, t, level, h).start()

        return h * 2

    lax.fori_loop(0, levels + 1, body, 1)

    def share(d, t):
        return pltpu.make_async_remote_copy(
            src_ref=x_ref.at[t],
            dst_ref=everyone[t].at[point],
            send_sem=gather_sems.at[0, d, t],
            recv_sem=gather_sems.at[1, d, t],
            device_id=(me, others[d]),
            device_id_type=MESH,
        )

    for t in range(TILES):
        for d in range(energies - 1):
            share(d, t).start()
    tiles = [x_ref[t] for t in range(TILES)]
    store_wide(green_ref, tiles)
    for t in range(TILES):
        everyone[t][point] = tiles[t]

    def finish(level, h):
        for t in range(TILES):
            for kind, ok in ((0, me + h < slabs), (1, me >= h)):

                @pl.when(ok)
                def _():
                    send(kind, t, level, h).wait_send()

                @pl.when(ok & (level < levels - 1))
                def _():
                    send(kind + 2, t, level, h).wait_send()

        return h * 2

    lax.fori_loop(0, levels, finish, 1)

    loads[3].wait()
    pairs = pairs_ref.shape[0]
    anharmonic = anharmonic_ref[...] * (1.0 / pairs)
    low = lanes_of(WIDTH) < 64
    outs = []
    for t in range(TILES):
        for d in range(energies - 1):
            share(d, t).wait()
        for e in range(energies):
            turned[t, e] = pltpu.roll(everyone[t][e], 64, 1)
        straight = crossed = jnp.zeros((WIDTH, 128), jnp.float32)
        for p in range(pairs):
            first = everyone[t][pairs_ref[p, 0]]
            straight = straight + first * everyone[t][pairs_ref[p, 1]]
            crossed = crossed + first * turned[t, pairs_ref[p, 1]]
        total = jnp.where(low, straight - pltpu.roll(straight, 64, 1), crossed + pltpu.roll(crossed, 64, 1))
        part = anharmonic[:, HALF * t : HALF * (t + 1)]
        outs.append(total * jnp.concatenate([part, part], 1))
    store_wide(out_ref, outs)


def shards(energy_sq, broadening, onsite, coupling, sigma_in, anharmonic, energy_pairs):
    slabs, energies = lax.axis_size("slab"), lax.axis_size("energy")
    levels = slabs.bit_length() - 1
    block = (TILES, WIDTH, 128)
    vmem = pl.BlockSpec(memory_space=pltpu.VMEM)
    smem = pl.BlockSpec(memory_space=pltpu.SMEM)
    hbm = pl.BlockSpec(memory_space=pltpu.HBM)
    square = pltpu.VMEM((WIDTH, WIDTH), jnp.float32)
    wide = jax.ShapeDtypeStruct((WIDTH, 2 * WIDTH), jnp.float32)
    buffer = pltpu.VMEM(block, jnp.float32)
    stack = pltpu.VMEM((levels,) + block, jnp.float32)
    green, sigma = pl.pallas_call(
        functools.partial(kernel, slabs, energies),
        out_shape=(wide, wide),
        in_specs=[smem, smem, hbm, hbm, hbm, hbm, smem],
        out_specs=(vmem, vmem),
        scratch_shapes=[square, square, pltpu.VMEM((WIDTH, 2 * WIDTH), jnp.float32), square]
        + [pltpu.SemaphoreType.DMA((4,)), square]
        + [buffer] * 2
        + [pltpu.VMEM((2, WIDTH, 4 * WIDTH), jnp.bfloat16)] * 2
        + [pltpu.VMEM((WIDTH, 2 * WIDTH), jnp.bfloat16)] * 2
        + [stack] * 6
        + [pltpu.VMEM((energies, WIDTH, 128), jnp.float32)] * TILES
        + [pltpu.VMEM((TILES, energies, WIDTH, 128), jnp.float32)]
        + [
            pltpu.SemaphoreType.DMA((2,)),
            pltpu.SemaphoreType.DMA((levels, 4, TILES)),
            pltpu.SemaphoreType.DMA((levels, 4, TILES)),
            pltpu.SemaphoreType.DMA((2, energies - 1, TILES)),
        ],
        compiler_params=pltpu.CompilerParams(
            collective_id=0, has_side_effects=True, vmem_limit_bytes=58 * 2**20
        ),
    )(energy_sq, broadening, onsite[0], coupling[0], sigma_in[0, 0], anharmonic[0], energy_pairs[0])
    return green[None, None], sigma[None, None]


def solution(mesh):
    in_specs = (
        P("energy"),
        P("energy"),
        P("slab", None, None),
        P("slab", None, None),
        P("energy", "slab", None, None),
        P("slab", None, None),
        P("energy", None, None),
    )
    out_specs = (P("energy", "slab", None, None), P("energy", "slab", None, None))
    return jax.shard_map(shards, mesh=mesh, in_specs=in_specs, out_specs=out_specs, check_vma=False)
```
